512 devices in a mesh: elem: 32 (over x, z_hi, core), range: 16 (over y, z_lo).
Axes of the slice: x: 4, y: 8, z: 8 (z_hi: 4, z_lo: 2; z = z_hi * 2 + z_lo), core: 2. Of those that a mesh axis runs over, the one named last changes fastest.
Arguments:
- echoes: bfloat16 [2, 4096, 32, 4096], P(None, 'elem', 'range'), may hold values from -6 to 6
- steer_table: bfloat16 [2, 128, 4096], P(None, None, 'elem'), may hold values from -0.0625 to 0.0625
- beam_index: int32 [64], replicated, may hold values from 0 to 127
- pulse_code: bfloat16 [2, 256], replicated, may hold values from -0.25 to 0.25
- clutter_taps: float32 [2, 2], replicated, may hold values from 0.3 to 0.9
- dilation: int32 [2], replicated, may hold values from 1 to 3, as said below
Outputs:
- filtered: float32 [64, 2, 32, 4096], P('elem', None, None, 'range')
The draws below stay inside these ranges and needn't reach their ends.
Inputs may be any that keep to these rules, and one draw needn't show every extreme that they name: `dilation`: the 2 sections have distinct spacings, the largest of them 3.
All inputs are finite; a program needn't handle non-finite values.
Results may differ from the reference program's by a relative error of at most 0.019.
Values may be sent and summed in bfloat16 or wider, within the bound.
No kernel may reach another device: no remote copies, remote signals or barrier semaphores. Data moves between devices by JAX's collectives and lax.ppermute only.
A program may use at most 64 MiB of HBM per device.

```python
import jax
import jax.numpy as jnp
from jax import lax

ELEMENTS = 4096
BEAMS = 64
TABLE = 128
TAPS = 256
SECTIONS = 2
PULSES = 32
GATES = 4096
N_ELEM = 32


def draw_dilation(key, part):
    key = jax.random.fold_in(key, 7)
    other_key, order_key = jax.random.split(key)
    shorter = jax.random.randint(other_key, (), 1, 3).astype(jnp.int32)
    flipped = jax.random.randint(order_key, (), 0, 2).astype(jnp.int32)
    longest = jnp.int32(3)
    first = jnp.where(flipped == 1, longest, shorter)
    second = jnp.where(flipped == 1, shorter, longest)
    return jnp.stack([first, second]).astype(jnp.int32)


def place_ends(drawn, stream_key, smallest, high):
    dims = drawn.shape
    index_at = [jax.random.randint(jax.random.fold_in(stream_key, axis), (), 0, dims[axis]) for axis in range(len(dims))]
    drawn = drawn.at[tuple(index_at)].set(smallest)
    longest = dims.index(max(dims))
    index_at[longest] = (index_at[longest] + 1) % dims[longest]
    return drawn.at[tuple(index_at)].set(high)


def shard_levels(own_key, shape, shards, low, largest):
    def one(position, parts):
        draws = jax.random.uniform(jax.random.fold_in(jax.random.fold_in(own_key, 6), position), (parts,), jnp.float32, low / len(shards), largest / len(shards))
        return jnp.repeat(jnp.exp(draws), shape[position] // parts).reshape((-1,) + (1,) * (len(shape) - position - 1))

    factor_of = one(*shards[0])
    for cut in shards[1:]:
        factor_of = factor_of * one(*cut)
    return factor_of


def bell_draw(stream_key, shape, deviation, bound, cuts=(), kind=jnp.bfloat16):
    drawn = jax.random.normal(stream_key, shape, jnp.float32) * deviation
    if len(cuts) > 0:
        drawn = shard_levels(stream_key, shape, cuts, -0.22, 0.18) * drawn
    return jnp.clip(drawn, min=-bound, max=bound).astype(kind)


def setup_inputs(seed: int = 0) -> dict:
    key_list = jax.random.split(jax.random.key(seed), 7)
    echoes = bell_draw(key_list[0], (2, ELEMENTS, PULSES, GATES), 1.0, 6.0, ((1, 32), (2, 16)))
    steer_table = bell_draw(key_list[1], (2, TABLE, ELEMENTS), (2 * ELEMENTS) ** -0.5, 0.0625, ((2, 32),))
    beam_index = place_ends(jax.random.randint(key_list[2], (BEAMS,), 0, TABLE), jax.random.fold_in(key_list[2], 1), 0, TABLE - 1).astype(jnp.int32)
    pulse_code = bell_draw(key_list[3], (2, TAPS), (2 * TAPS) ** -0.5, 0.25)
    clutter_taps = jnp.clip(jax.random.uniform(key_list[4], (SECTIONS, 2), jnp.float32, 0.3, 0.9), 0.3, 0.9)
    dilation = draw_dilation(jax.random.fold_in(key_list[6], 71), 0)
    return {"echoes": echoes, "steer_table": steer_table, "beam_index": beam_index, "pulse_code": pulse_code, "clutter_taps": clutter_taps, "dilation": dilation}


def delayed(values, spacing):
    pulse_count = values.shape[2]
    rolled = jnp.roll(values, spacing, axis=2)
    inside = (jnp.arange(pulse_count, dtype=jnp.int32) >= spacing)[:, None]
    return jnp.where(inside, rolled, jnp.zeros_like(rolled))


def reference(echoes, steer_table, beam_index, pulse_code, clutter_taps, dilation):
    weights = jnp.take(steer_table, beam_index, axis=1)
    group_size = ELEMENTS // N_ELEM
    pulse_count = echoes.shape[2]
    gate_count = echoes.shape[3]

    def group_term(accum, group_index):
        first = (group_index * group_size).astype(jnp.int32)
        part_w = lax.dynamic_slice_in_dim(weights, first, group_size, 2)
        real_w = part_w[0]
        imag_w = part_w[1]
        stacked = jnp.stack([jnp.concatenate([real_w, -imag_w], 1), jnp.concatenate([imag_w, real_w], 1)], 1)
        stacked = stacked.reshape(2 * BEAMS, 2 * group_size)
        samples = lax.dynamic_slice_in_dim(echoes, first, group_size, 1).reshape(2 * group_size, pulse_count * gate_count)
        term = jnp.dot(stacked, samples, preferred_element_type=jnp.float32)
        rounded = lax.optimization_barrier(term.astype(jnp.bfloat16))
        return accum + rounded.astype(jnp.float32), None

    total, unused = lax.scan(group_term, jnp.zeros((2 * BEAMS, pulse_count * gate_count), jnp.float32), jnp.arange(N_ELEM, dtype=jnp.int32))
    signal = total.astype(jnp.bfloat16).reshape(BEAMS, 2, pulse_count, gate_count).astype(jnp.float32)
    padded = jnp.pad(signal, ((0, 0), (0, 0), (0, 0), (0, TAPS)))
    code = pulse_code.astype(jnp.float32)

    def add_tap(tap_index, sums):
        where_at = jnp.asarray(tap_index).astype(jnp.int32)
        shifted = lax.dynamic_slice_in_dim(padded, where_at, gate_count, 3)
        code_real = lax.dynamic_index_in_dim(code[0], where_at, keepdims=False)
        code_imag = lax.dynamic_index_in_dim(code[1], where_at, keepdims=False)
        real_sum = sums[0] + code_real * shifted[:, 0] + code_imag * shifted[:, 1]
        imag_sum = sums[1] + code_real * shifted[:, 1] - code_imag * shifted[:, 0]
        return (real_sum, imag_sum)

    start_sums = (jnp.zeros((BEAMS, pulse_count, gate_count), jnp.float32), jnp.zeros((BEAMS, pulse_count, gate_count), jnp.float32))
    real_sum, imag_sum = lax.fori_loop(0, TAPS, add_tap, start_sums)
    filtered = jnp.stack([real_sum, imag_sum], 1)
    for section_index in range(SECTIONS):
        spacing = dilation[section_index]
        filtered = filtered - clutter_taps[section_index, 0] * delayed(filtered, spacing) - clutter_taps[section_index, 1] * delayed(filtered, 2 * spacing)
    return filtered
```

```python
import jax
import jax.numpy as jnp
from jax import lax
from jax.experimental import pallas as pl
from jax.experimental.pallas import tpu as pltpu
from jax.sharding import Mesh, PartitionSpec as P

bf16, f32, i32 = jnp.bfloat16, jnp.float32, jnp.int32
LANES = 128
PAIR = 8
VMEM_BYTES = 60 << 20
SMALL_VMEM_BYTES = 24 << 20
FIRST = (((0,), (0,)), ((), ()))
LAST = (((1,), (1,)), ((), ()))


def iota(shape, dim):
    return lax.broadcasted_iota(i32, shape, dim)


def one_hot(condition):
    return condition.astype(f32).astype(bf16)


def steering(core, table_ref, index_ref, rows):
    elems = table_ref.shape[2]
    beams = index_ref.shape[1]
    select = one_hot(index_ref[...] == iota((table_ref.shape[1], beams), 0))
    row = iota((rows, beams), 0)
    half = lax.div(row, rows // 2)
    within = lax.rem(row, rows // 2)
    owner = jnp.where(half == 1, core, 1 - core)
    beam = lax.div(within, PAIR) * 4 + owner * 2 + lax.div(lax.rem(within, PAIR), 4)
    pick = one_hot(beam == iota((rows, beams), 1))
    parts = []
    for part in range(2):
        chosen = lax.dot_general(select, table_ref[part], FIRST, preferred_element_type=f32)
        parts.append(jnp.dot(pick, chosen.astype(bf16), preferred_element_type=f32))
    imag = lax.rem(lax.div(iota((rows, elems), 0), 2), 2) == 1
    by_real = jnp.where(imag, parts[1], parts[0]).astype(bf16)
    by_imag = jnp.where(imag, parts[0], -parts[1]).astype(bf16)
    widen = one_hot(lax.div(iota((elems, 2 * elems), 1), 2) == iota((elems, 2 * elems), 0))
    same_pulse = lax.rem(iota((rows, 2 * elems), 0), 2) == lax.rem(iota((rows, 2 * elems), 1), 2)
    wide = [
        jnp.where(same_pulse, jnp.dot(m, widen, preferred_element_type=f32), 0.0).astype(bf16)
        for m in (by_real, by_imag)
    ]
    return jnp.concatenate(wide, 1)


def beamform_kernel(index_ref, echo_ref, table_ref, other_ref, own_ref, weight_ref):
    rows = weight_ref.shape[0]

    @pl.when(pl.program_id(0) == 0)
    def _():
        weight_ref[...] = steering(lax.axis_index("c"), table_ref, index_ref, rows)

    samples = echo_ref[...].reshape(-1, echo_ref.shape[3])
    partial = jnp.dot(weight_ref[...], samples, preferred_element_type=f32).astype(bf16)
    other_ref[...] = partial[: rows // 2]
    own_ref[...] = partial[rows // 2 :]


def beamform(echoes, steer_table, beam_index):
    steps = 2
    _, elems, pulses, gates = echoes.shape
    beams = beam_index.shape[0]
    rows = 2 * beams * pulses
    width = gates // steps
    return pl.pallas_call(
        beamform_kernel,
        grid=(steps,),
        in_specs=[
            pl.BlockSpec((1, beams), lambda i: (0, 0)),
            pl.BlockSpec((2, elems, pulses, width), lambda i: (0, 0, 0, i)),
            pl.BlockSpec(steer_table.shape, lambda i: (0, 0, 0)),
        ],
        out_specs=[pl.BlockSpec((rows // 2, width), lambda i: (0, i))] * 2,
        out_shape=[jax.ShapeDtypeStruct((rows // 2, gates), bf16)] * 2,
        scratch_shapes=[pltpu.VMEM((rows, 4 * elems), bf16)],
        compiler_params=pltpu.CompilerParams(vmem_limit_bytes=VMEM_BYTES),
    )(beam_index.reshape(1, beams), echoes, steer_table)


def compress_kernel(own_ref, came_ref, code_ref, out_ref, signal_ref, turned_ref):
    rows, gates = own_ref.shape
    taps = code_ref.shape[1]
    row, column = iota((rows, rows), 0), iota((rows, rows), 1)
    imag = lax.rem(lax.div(row, 2), 2) == 1
    turn = jnp.where(imag, -(column == row - 2).astype(f32), (column == row + 2).astype(f32)).astype(bf16)
    signal = (own_ref[...].astype(f32) + came_ref[...].astype(f32)).astype(bf16)
    signal_ref[:, :gates] = signal
    signal_ref[:, gates:] = jnp.zeros((rows, taps), bf16)
    turned_ref[:, :gates] = jnp.dot(turn, signal, preferred_element_type=f32).astype(bf16)
    turned_ref[:, gates:] = jnp.zeros((rows, taps), bf16)
    bands = []
    for part in range(2):
        code = code_ref[part : part + 1, :].astype(f32)
        code = jnp.concatenate([code, jnp.zeros_like(code)], 1)
        code = jnp.broadcast_to(code, (taps, 2 * taps))
        bands.append(pltpu.roll(code, 0, 1, stride=1, stride_axis=0).astype(bf16))
    for slab in range(gates // taps):
        here = slice(slab * taps, (slab + 2) * taps)
        total = lax.dot_general(signal_ref[:, here], bands[0], LAST, preferred_element_type=f32)
        total += lax.dot_general(turned_ref[:, here], bands[1], LAST, preferred_element_type=f32)
        total = total.reshape(rows // PAIR, PAIR, taps)
        total = jnp.concatenate([total[:, :, :LANES], total[:, :, LANES:]], 1)
        out_ref[:, slab] = total.astype(bf16)


def compress(own, came, pulse_code):
    rows, gates = own.shape
    taps = pulse_code.shape[1]
    return pl.pallas_call(
        compress_kernel,
        out_shape=jax.ShapeDtypeStruct((rows // PAIR, gates // taps, 2 * PAIR, LANES), bf16),
        scratch_shapes=[pltpu.VMEM((rows, gates + taps), bf16)] * 2,
        compiler_params=pltpu.CompilerParams(vmem_limit_bytes=SMALL_VMEM_BYTES),
    )(own, came, pulse_code)


def delayed(value, spacing):
    rolled = pltpu.roll(value, spacing, 0)
    return jnp.where(iota(value.shape, 0) >= spacing, rolled, 0.0)


def filter_kernel(taps_ref, dilation_ref, parts_ref, out_ref, sum_ref):
    count, pairs = parts_ref.shape[:2]
    planes = sum_ref.shape[0]
    for pair in range(pairs):
        total = parts_ref[0, pair].astype(f32)
        for source in range(1, count):
            total += parts_ref[source, pair].astype(f32)
        for side in range(2):
            for plane in range(planes):
                row = side * PAIR + 2 * plane
                sum_ref[plane, 2 * pair : 2 * pair + 2, side * LANES : (side + 1) * LANES] = total[row : row + 2]
    for plane in range(planes):
        value = sum_ref[plane]
        for section in range(2):
            spacing = dilation_ref[section]
            near = taps_ref[section, 0] * delayed(value, spacing)
            far = taps_ref[section, 1] * delayed(value, 2 * spacing)
            value = value - near - far
        out_ref[plane] = value


def clutter_filter(parts, clutter_taps, dilation):
    pulses = 2 * parts.shape[1]
    planes = PAIR // 2
    width = 2 * LANES
    scalar = pl.BlockSpec(memory_space=pltpu.SMEM)
    return pl.pallas_call(
        filter_kernel,
        in_specs=[scalar, scalar, pl.BlockSpec(memory_space=pltpu.VMEM)],
        out_shape=jax.ShapeDtypeStruct((planes, pulses, width), f32),
        scratch_shapes=[pltpu.VMEM((planes, pulses, width), f32)],
        compiler_params=pltpu.CompilerParams(vmem_limit_bytes=SMALL_VMEM_BYTES),
    )(clutter_taps, dilation, parts)


def on_device(echoes, steer_table, beam_index, pulse_code, clutter_taps, dilation):
    x_count, z_count = lax.axis_size("x"), lax.axis_size("z")
    slabs = lax.axis_size("y") * lax.axis_size("w")
    other, own = beamform(echoes, steer_table, beam_index)
    came = lax.ppermute(other, "c", [(0, 1), (1, 0)])
    blocks = compress(own, came, pulse_code)
    blocks = blocks.reshape(x_count, z_count * slabs, 2 * PAIR, LANES)
    blocks = lax.all_to_all(blocks, "x", 0, 0)
    blocks = jnp.sum(blocks.astype(f32), 0).astype(bf16)
    blocks = lax.all_to_all(blocks, ("z", "y", "w"), 0, 0)
    blocks = blocks.reshape(z_count, slabs, 2 * PAIR, LANES)
    planes = clutter_filter(blocks, clutter_taps, dilation)
    return planes.reshape(2, 2, planes.shape[1], planes.shape[2])


def solution(mesh):
    split = Mesh(mesh.devices.reshape(4, 4, 2, 8, 2), ("x", "z", "c", "y", "w"))
    elem, gates = ("x", "z", "c"), ("y", "w")
    return jax.shard_map(
        on_device,
        mesh=split,
        in_specs=(P(None, elem, gates, None), P(None, None, elem), P(), P(), P(), P()),
        out_specs=P(elem, None, None, gates),
        check_vma=False,
    )
```

```python
import jax
import jax.numpy as jnp
from jax import lax
from jax.experimental import pallas as pl
from jax.experimental.pallas import tpu as pltpu
from jax.sharding import Mesh, PartitionSpec as P

bf16, f32, i32 = jnp.bfloat16, jnp.float32, jnp.int32
LANES = 128
PAIR = 8
VMEM_BYTES = 24 << 20
ECHO_STEPS = 4
FIRST = (((0,), (0,)), ((), ()))
LAST = (((1,), (1,)), ((), ()))


def iota(shape, dim):
    return lax.broadcasted_iota(i32, shape, dim)


def one_hot(condition):
    return condition.astype(f32).astype(bf16)


def steering(table_ref, index_ref, rows):
    core = lax.axis_index("c")
    elems = table_ref.shape[2]
    beams = index_ref.shape[1]
    select = one_hot(index_ref[...] == iota((table_ref.shape[1], beams), 0))
    row = iota((rows, beams), 0)
    half = lax.div(row, rows // 2)
    within = lax.rem(row, rows // 2)
    owner = jnp.where(half == 1, core, 1 - core)
    beam = lax.div(within, PAIR) * 4 + owner * 2 + lax.div(lax.rem(within, PAIR), 4)
    pick = one_hot(beam == iota((rows, beams), 1))
    parts = []
    for part in range(2):
        chosen = lax.dot_general(select, table_ref[part], FIRST, preferred_element_type=f32)
        parts.append(jnp.dot(pick, chosen.astype(bf16), preferred_element_type=f32))
    imag = lax.rem(lax.div(iota((rows, elems), 0), 2), 2) == 1
    by_real = jnp.where(imag, parts[1], parts[0]).astype(bf16)
    by_imag = jnp.where(imag, parts[0], -parts[1]).astype(bf16)
    widen = one_hot(lax.div(iota((elems, 2 * elems), 1), 2) == iota((elems, 2 * elems), 0))
    same_pulse = lax.rem(iota((rows, 2 * elems), 0), 2) == lax.rem(iota((rows, 2 * elems), 1), 2)
    wide = [
        jnp.where(same_pulse, jnp.dot(m, widen, preferred_element_type=f32), 0.0).astype(bf16)
        for m in (by_real, by_imag)
    ]
    return jnp.concatenate(wide, 1)


def beamform_kernel(index_hbm, table_hbm, echo_hbm, other_ref, own_ref, index_ref, table_ref, echo_ref, done):
    rows = 2 * other_ref.shape[0]
    pulses, gates = echo_hbm.shape[2:]
    width = gates // ECHO_STEPS
    small = [
        pltpu.make_async_copy(index_hbm, index_ref, done.at[ECHO_STEPS]),
        pltpu.make_async_copy(table_hbm, table_ref, done.at[ECHO_STEPS + 1]),
    ]
    spans = [slice(step * width, (step + 1) * width) for step in range(ECHO_STEPS)]
    large = [
        pltpu.make_async_copy(echo_hbm.at[:, :, :, span], echo_ref.at[:, :, :, span], done.at[step])
        for step, span in enumerate(spans)
    ]
    for copy in small + large:
        copy.start()
    for copy in small:
        copy.wait()
    weights = steering(table_ref, index_ref, rows)
    for span, copy in zip(spans, large):
        copy.wait()
        samples = echo_ref[:, :, :, span].reshape(-1, width)
        partial = jnp.dot(weights, samples, preferred_element_type=f32).astype(bf16)
        other_ref[:, span] = partial[: rows // 2]
        own_ref[:, span] = partial[rows // 2 :]


def beamform(echoes, steer_table, beam_index):
    _, elems, pulses, gates = echoes.shape
    beams = beam_index.shape[0]
    rows = 2 * beams * pulses
    operands = (beam_index.reshape(1, beams), steer_table, echoes)
    return pl.pallas_call(
        beamform_kernel,
        in_specs=[pl.BlockSpec(memory_space=pltpu.HBM)] * 3,
        out_specs=[pl.BlockSpec(memory_space=pltpu.VMEM)] * 2,
        out_shape=[jax.ShapeDtypeStruct((rows // 2, gates), bf16)] * 2,
        scratch_shapes=[
            pltpu.VMEM((1, beams), i32),
            pltpu.VMEM(steer_table.shape, bf16),
            pltpu.VMEM(echoes.shape, bf16),
            pltpu.SemaphoreType.DMA((ECHO_STEPS + 2,)),
        ],
        compiler_params=pltpu.CompilerParams(vmem_limit_bytes=VMEM_BYTES),
    )(*(pltpu.with_memory_space_constraint(a, pltpu.HBM) for a in operands))


def band_kernel(code_ref, band_ref):
    taps = code_ref.shape[1]
    for part in range(2):
        code = code_ref[part : part + 1, :].astype(f32)
        code = jnp.concatenate([code, jnp.zeros_like(code)], 1)
        code = jnp.broadcast_to(code, (taps, 2 * taps))
        band_ref[part] = pltpu.roll(code, 0, 1, stride=1, stride_axis=0).astype(bf16)


def toeplitz_bands(pulse_code):
    taps = pulse_code.shape[1]
    return pl.pallas_call(
        band_kernel,
        out_shape=jax.ShapeDtypeStruct((2, taps, 2 * taps), bf16),
        compiler_params=pltpu.CompilerParams(vmem_limit_bytes=VMEM_BYTES),
        cost_estimate=pl.CostEstimate(flops=1 << 22, bytes_accessed=1 << 22, transcendentals=0),
    )(pulse_code)


def compress_kernel(own_ref, came_ref, band_ref, out_ref):
    chunks, chips, slabs = out_ref.shape[:3]
    taps = band_ref.shape[1]
    rows = chips * PAIR
    past = jnp.zeros((rows, taps), bf16)
    for chunk in range(chunks):
        here = slice(chunk * rows, (chunk + 1) * rows)
        signal = own_ref[here].astype(f32) + came_ref[here].astype(f32)
        imag = lax.rem(lax.div(iota(signal.shape, 0), 2), 2) == 1
        turned = jnp.where(imag, -pltpu.roll(signal, 2, 0), pltpu.roll(signal, rows - 2, 0))
        total = None
        for part, values in enumerate((signal, turned)):
            values = jnp.concatenate([values.astype(bf16), past], 1)
            windows = [values[:, slab * taps : (slab + 2) * taps] for slab in range(slabs)]
            windows = jnp.concatenate(windows, 0)
            product = lax.dot_general(windows, band_ref[part], LAST, preferred_element_type=f32)
            total = product if total is None else total + product
        total = total.reshape(slabs, chips, PAIR, taps)
        for slab in range(slabs):
            block = total[slab]
            out_ref[chunk, :, slab] = jnp.concatenate([block[:, :, :LANES], block[:, :, LANES:]], 1).astype(bf16)


def compress(own, came, bands, chunks):
    rows, gates = own.shape
    taps = bands.shape[1]
    shape = (chunks, rows // PAIR // chunks, gates // taps, 2 * PAIR, LANES)
    return pl.pallas_call(
        compress_kernel,
        out_shape=jax.ShapeDtypeStruct(shape, bf16),
        compiler_params=pltpu.CompilerParams(vmem_limit_bytes=VMEM_BYTES),
    )(own, came, bands)


def sum_kernel(parts_ref, out_ref):
    total = parts_ref[0].astype(f32)
    for source in range(1, parts_ref.shape[0]):
        total += parts_ref[source].astype(f32)
    out_ref[...] = total.astype(bf16)


def summed(parts):
    return pl.pallas_call(
        sum_kernel,
        out_shape=jax.ShapeDtypeStruct(parts.shape[1:], bf16),
        compiler_params=pltpu.CompilerParams(vmem_limit_bytes=VMEM_BYTES),
    )(parts)


def delayed(value, spacing):
    rolled = pltpu.roll(value, spacing, 0)
    return jnp.where(iota(value.shape, 0) >= spacing, rolled, 0.0)


def filter_kernel(taps_ref, dilation_ref, parts_ref, out_ref, sum_ref):
    count, pairs = parts_ref.shape[:2]
    planes = sum_ref.shape[0]
    for pair in range(pairs):
        total = parts_ref[0, pair].astype(f32)
        for source in range(1, count):
            total += parts_ref[source, pair].astype(f32)
        for side in range(2):
            for plane in range(planes):
                row = side * PAIR + 2 * plane
                sum_ref[plane, 2 * pair : 2 * pair + 2, side * LANES : (side + 1) * LANES] = total[row : row + 2]
    for plane in range(planes):
        value = sum_ref[plane]
        for section in range(2):
            spacing = dilation_ref[section]
            near = taps_ref[section, 0] * delayed(value, spacing)
            far = taps_ref[section, 1] * delayed(value, 2 * spacing)
            value = value - near - far
        out_ref[plane] = value


def clutter_filter(parts, clutter_taps, dilation):
    pulses = 2 * parts.shape[1]
    planes = PAIR // 2
    width = 2 * LANES
    scalar = pl.BlockSpec(memory_space=pltpu.SMEM)
    return pl.pallas_call(
        filter_kernel,
        in_specs=[scalar, scalar, pl.BlockSpec(memory_space=pltpu.VMEM)],
        out_shape=jax.ShapeDtypeStruct((planes, pulses, width), f32),
        scratch_shapes=[pltpu.VMEM((planes, pulses, width), f32)],
        compiler_params=pltpu.CompilerParams(vmem_limit_bytes=VMEM_BYTES),
    )(clutter_taps, dilation, parts)


def on_device(echoes, steer_table, beam_index, pulse_code, clutter_taps, dilation):
    x_count, z_count = lax.axis_size("x"), lax.axis_size("z")
    slabs = lax.axis_size("y") * lax.axis_size("w")
    other, own = beamform(echoes, steer_table, beam_index)
    came = lax.ppermute(other, "c", [(0, 1), (1, 0)])
    bands = toeplitz_bands(pulse_code)
    blocks = compress(own, came, bands, x_count)
    blocks = summed(lax.all_to_all(blocks, "x", 0, 0)).reshape(z_count * slabs, 2 * PAIR, LANES)
    blocks = lax.all_to_all(blocks, ("z", "y", "w"), 0, 0)
    blocks = blocks.reshape(z_count, slabs, 2 * PAIR, LANES)
    planes = clutter_filter(blocks, clutter_taps, dilation)
    return planes.reshape(2, 2, planes.shape[1], planes.shape[2])


def solution(mesh):
    split = Mesh(mesh.devices.reshape(4, 4, 2, 8, 2), ("x", "z", "c", "y", "w"))
    elem, gates = ("x", "z", "c"), ("y", "w")
    return jax.shard_map(
        on_device,
        mesh=split,
        in_specs=(P(None, elem, gates, None), P(None, None, elem), P(), P(), P(), P()),
        out_specs=P(elem, None, None, gates),
        check_vma=False,
    )
```

```python
import jax
import jax.numpy as jnp
from jax import lax
from jax.experimental import pallas as pl
from jax.experimental.pallas import tpu as pltpu
from jax.sharding import Mesh, PartitionSpec as P

bf16, f32, i32 = jnp.bfloat16, jnp.float32, jnp.int32
LANES = 128
PAIR = 8
VMEM_BYTES = 24 << 20
ECHO_STEPS = 2
FIRST = (((0,), (0,)), ((), ()))
LAST = (((1,), (1,)), ((), ()))


def iota(shape, dim):
    return lax.broadcasted_iota(i32, shape, dim)


def one_hot(condition):
    return condition.astype(f32).astype(bf16)


def steering(table_ref, index_ref, rows, core):
    elems = table_ref.shape[2]
    beams = index_ref.shape[1]
    select = one_hot(index_ref[...] == iota((table_ref.shape[1], beams), 0))
    row = iota((rows, beams), 0)
    beam = lax.div(row, PAIR) * 4 + core * 2 + lax.rem(lax.div(row, 2), 2)
    pick = one_hot(beam == iota((rows, beams), 1))
    parts = []
    for part in range(2):
        chosen = lax.dot_general(select, table_ref[part], FIRST, preferred_element_type=f32)
        parts.append(jnp.dot(pick, chosen.astype(bf16), preferred_element_type=f32))
    imag = lax.rem(iota((rows, elems), 0), 2) == 1
    by_real = jnp.where(imag, parts[1], parts[0]).astype(bf16)
    by_imag = jnp.where(imag, parts[0], -parts[1]).astype(bf16)
    widen = one_hot(lax.div(iota((elems, 2 * elems), 1), 2) == iota((elems, 2 * elems), 0))
    same_pulse = lax.div(lax.rem(iota((rows, 2 * elems), 0), PAIR), 4) == lax.rem(iota((rows, 2 * elems), 1), 2)
    wide = [
        jnp.where(same_pulse, jnp.dot(m, widen, preferred_element_type=f32), 0.0).astype(bf16)
        for m in (by_real, by_imag)
    ]
    return jnp.concatenate(wide, 1)


def beam_chunk(weights, echo_ref, span):
    samples = echo_ref[:, :, :, span].reshape(weights.shape[1], -1)
    return jnp.dot(weights, samples, preferred_element_type=f32).astype(bf16)


def other_kernel(index_hbm, table_hbm, echo_hbm, other_ref, index_ref, table_ref, echo_ref, done):
    gates = echo_hbm.shape[3]
    width = gates // ECHO_STEPS
    small = [
        pltpu.make_async_copy(index_hbm, index_ref, done.at[ECHO_STEPS]),
        pltpu.make_async_copy(table_hbm, table_ref, done.at[ECHO_STEPS + 1]),
    ]
    spans = [slice(step * width, (step + 1) * width) for step in range(ECHO_STEPS)]
    large = [
        pltpu.make_async_copy(echo_hbm.at[:, :, :, span], echo_ref.at[:, :, :, span], done.at[step])
        for step, span in enumerate(spans)
    ]
    for copy in small + large:
        copy.start()
    for copy in small:
        copy.wait()
    weights = steering(table_ref, index_ref, other_ref.shape[0], 1 - lax.axis_index("c"))
    for span, copy in zip(spans, large):
        copy.wait()
        other_ref[:, span] = beam_chunk(weights, echo_ref, span)


def own_kernel(index_ref, table_ref, echo_ref, own_ref):
    gates = own_ref.shape[1]
    width = gates // ECHO_STEPS
    weights = steering(table_ref, index_ref, own_ref.shape[0], lax.axis_index("c"))
    for step in range(ECHO_STEPS):
        span = slice(step * width, (step + 1) * width)
        own_ref[:, span] = beam_chunk(weights, echo_ref, span)


def beamform(echoes, steer_table, beam_index):
    _, _, pulses, gates = echoes.shape
    beams = beam_index.shape[0]
    partial = jax.ShapeDtypeStruct((beams * pulses, gates), bf16)
    operands = (beam_index.reshape(1, beams), steer_table, echoes)
    near = pl.BlockSpec(memory_space=pltpu.VMEM)
    other, *held = pl.pallas_call(
        other_kernel,
        in_specs=[pl.BlockSpec(memory_space=pltpu.HBM)] * 3,
        out_specs=[near] * 4,
        out_shape=[partial] + [jax.ShapeDtypeStruct(a.shape, a.dtype) for a in operands],
        scratch_shapes=[pltpu.SemaphoreType.DMA((ECHO_STEPS + 2,))],
        compiler_params=pltpu.CompilerParams(vmem_limit_bytes=VMEM_BYTES),
    )(*(pltpu.with_memory_space_constraint(a, pltpu.HBM) for a in operands))

    def own():
        return pl.pallas_call(
            own_kernel,
            in_specs=[near] * 3,
            out_specs=near,
            out_shape=partial,
            compiler_params=pltpu.CompilerParams(vmem_limit_bytes=VMEM_BYTES),
            cost_estimate=pl.CostEstimate(flops=1 << 30, bytes_accessed=1 << 22, transcendentals=0),
        )(*held)

    return other, own


def band_kernel(code_ref, band_ref):
    taps = code_ref.shape[1]
    for part in range(2):
        code = code_ref[part : part + 1, :].astype(f32)
        code = jnp.concatenate([code, jnp.zeros_like(code)], 1)
        code = jnp.broadcast_to(code, (taps, 2 * taps))
        band_ref[part] = pltpu.roll(code, 0, 1, stride=1, stride_axis=0).astype(bf16)


def toeplitz_bands(pulse_code):
    taps = pulse_code.shape[1]
    return pl.pallas_call(
        band_kernel,
        out_shape=jax.ShapeDtypeStruct((2, taps, 2 * taps), bf16),
        compiler_params=pltpu.CompilerParams(vmem_limit_bytes=VMEM_BYTES),
        cost_estimate=pl.CostEstimate(flops=1 << 22, bytes_accessed=1 << 22, transcendentals=0),
    )(pulse_code)


def add_kernel(own_ref, came_ref, out_ref):
    rows = out_ref.shape[1]
    for chunk in range(out_ref.shape[0]):
        here = slice(chunk * rows, (chunk + 1) * rows)
        out_ref[chunk] = (own_ref[here].astype(f32) + came_ref[here].astype(f32)).astype(bf16)


def added(own, came, chunks):
    rows, gates = own.shape
    return pl.pallas_call(
        add_kernel,
        out_shape=jax.ShapeDtypeStruct((chunks, rows // chunks, gates), bf16),
        compiler_params=pltpu.CompilerParams(vmem_limit_bytes=VMEM_BYTES),
    )(own, came)


def compress_kernel(parts_ref, band_ref, out_ref):
    sources, rows, _ = parts_ref.shape
    chips, slabs = out_ref.shape[:2]
    taps = band_ref.shape[1]
    signal = parts_ref[0].astype(f32)
    for source in range(1, sources):
        signal += parts_ref[source].astype(f32)
    imag = lax.rem(iota(signal.shape, 0), 2) == 1
    turned = jnp.where(imag, -pltpu.roll(signal, 1, 0), pltpu.roll(signal, rows - 1, 0))
    past = jnp.zeros((rows, taps), bf16)
    total = None
    for part, values in enumerate((signal, turned)):
        values = jnp.concatenate([values.astype(bf16), past], 1)
        windows = [values[:, slab * taps : (slab + 2) * taps] for slab in range(slabs)]
        windows = jnp.concatenate(windows, 0)
        product = lax.dot_general(windows, band_ref[part], LAST, preferred_element_type=f32)
        total = product if total is None else total + product
    total = total.reshape(slabs, chips, PAIR, taps)
    for slab in range(slabs):
        block = total[slab]
        out_ref[:, slab] = jnp.concatenate([block[:, :, :LANES], block[:, :, LANES:]], 1).astype(bf16)


def compress(parts, bands):
    _, rows, gates = parts.shape
    taps = bands.shape[1]
    return pl.pallas_call(
        compress_kernel,
        out_shape=jax.ShapeDtypeStruct((rows // PAIR, gates // taps, 2 * PAIR, LANES), bf16),
        compiler_params=pltpu.CompilerParams(vmem_limit_bytes=VMEM_BYTES),
    )(parts, bands)


def delays(value, spacing):
    rows, width = value.shape
    planes = PAIR // 2
    zeros = jnp.zeros((PAIR, width), f32)
    padded = jnp.concatenate([zeros, zeros, zeros, value], 0)
    turned = pltpu.roll(padded, planes, 0)

    def late(pulses):
        source, first = (padded, 3 * PAIR - pulses * planes) if pulses % 2 == 0 else (turned, 3 * PAIR - (pulses - 1) * planes)
        return source[first : first + rows]

    near = jnp.where(spacing == 1, late(1), jnp.where(spacing == 2, late(2), late(3)))
    far = jnp.where(spacing == 1, late(2), jnp.where(spacing == 2, late(4), late(6)))
    return near, far


def filter_kernel(taps_ref, dilation_ref, parts_ref, out_ref, value_ref):
    count, pairs = parts_ref.shape[:2]
    planes, pulses = out_ref.shape[:2]
    total = parts_ref[0].astype(f32)
    for source in range(1, count):
        total += parts_ref[source].astype(f32)
    for side in range(2):
        value = total[:, side * PAIR : (side + 1) * PAIR].reshape(pairs * PAIR, LANES)
        for section in range(2):
            near, far = delays(value, dilation_ref[section])
            value = value - taps_ref[section, 0] * near - taps_ref[section, 1] * far
        value_ref[...] = value
        for plane in range(planes):
            out_ref[plane, :, side * LANES : (side + 1) * LANES] = value_ref[pl.ds(plane, pulses, stride=planes), :]


def clutter_filter(parts, clutter_taps, dilation):
    pulses = 2 * parts.shape[1]
    planes = PAIR // 2
    scalar = pl.BlockSpec(memory_space=pltpu.SMEM)
    return pl.pallas_call(
        filter_kernel,
        in_specs=[scalar, scalar, pl.BlockSpec(memory_space=pltpu.VMEM)],
        out_shape=jax.ShapeDtypeStruct((planes, pulses, 2 * LANES), f32),
        scratch_shapes=[pltpu.VMEM((pulses * planes, LANES), f32)],
        compiler_params=pltpu.CompilerParams(vmem_limit_bytes=VMEM_BYTES),
    )(clutter_taps, dilation, parts)


def on_device(echoes, steer_table, beam_index, pulse_code, clutter_taps, dilation):
    x_count, z_count = lax.axis_size("x"), lax.axis_size("z")
    slabs = lax.axis_size("y") * lax.axis_size("w")
    other, own = beamform(echoes, steer_table, beam_index)
    came = lax.ppermute(other, "c", [(0, 1), (1, 0)])
    own = own()
    bands = toeplitz_bands(pulse_code)
    came, bands = lax.optimization_barrier((came, bands))
    parts = lax.all_to_all(added(own, came, x_count), "x", 0, 0)
    blocks = compress(parts, bands).reshape(z_count * slabs, 2 * PAIR, LANES)
    blocks = lax.all_to_all(blocks, ("z", "y", "w"), 0, 0)
    blocks = blocks.reshape(z_count, slabs, 2 * PAIR, LANES)
    planes = clutter_filter(blocks, clutter_taps, dilation)
    return planes.reshape(2, 2, planes.shape[1], planes.shape[2])


def solution(mesh):
    split = Mesh(mesh.devices.reshape(4, 4, 2, 8, 2), ("x", "z", "c", "y", "w"))
    elem, gates = ("x", "z", "c"), ("y", "w")
    return jax.shard_map(
        on_device,
        mesh=split,
        in_specs=(P(None, elem, gates, None), P(None, None, elem), P(), P(), P(), P()),
        out_specs=P(elem, None, None, gates),
        check_vma=False,
    )
```

```python
import jax
import jax.numpy as jnp
from jax import lax
from jax.experimental import pallas as pl
from jax.experimental.pallas import tpu as pltpu
from jax.sharding import Mesh, PartitionSpec as P

bf16, f32, i32 = jnp.bfloat16, jnp.float32, jnp.int32
LANES = 128
PAIR = 8
VMEM_BYTES = 24 << 20
ECHO_STEPS = 2
FIRST = (((0,), (0,)), ((), ()))
LAST = (((1,), (1,)), ((), ()))


def iota(shape, dim):
    return lax.broadcasted_iota(i32, shape, dim)


def one_hot(condition):
    return condition.astype(f32).astype(bf16)


def steering(table_ref, index_ref, rows, core):
    elems = table_ref.shape[2]
    beams = index_ref.shape[1]
    select = one_hot(index_ref[...] == iota((table_ref.shape[1], beams), 0))
    row = iota((rows, beams), 0)
    beam = lax.div(row, PAIR) * 4 + core * 2 + lax.rem(lax.div(row, 2), 2)
    pick = one_hot(beam == iota((rows, beams), 1))
    parts = []
    for part in range(2):
        chosen = lax.dot_general(select, table_ref[part], FIRST, preferred_element_type=f32)
        parts.append(jnp.dot(pick, chosen.astype(bf16), preferred_element_type=f32))
    imag = lax.rem(iota((rows, elems), 0), 2) == 1
    by_real = jnp.where(imag, parts[1], parts[0]).astype(bf16)
    by_imag = jnp.where(imag, parts[0], -parts[1]).astype(bf16)
    widen = one_hot(lax.div(iota((elems, 2 * elems), 1), 2) == iota((elems, 2 * elems), 0))
    same_pulse = lax.div(lax.rem(iota((rows, 2 * elems), 0), PAIR), 4) == lax.rem(iota((rows, 2 * elems), 1), 2)
    wide = [
        jnp.where(same_pulse, jnp.dot(m, widen, preferred_element_type=f32), 0.0).astype(bf16)
        for m in (by_real, by_imag)
    ]
    return jnp.concatenate(wide, 1)


def beam_chunk(weights, echo_ref, span):
    samples = echo_ref[:, :, :, span].reshape(weights.shape[1], -1)
    return jnp.dot(weights, samples, preferred_element_type=f32).astype(bf16)


def other_kernel(index_hbm, table_hbm, echo_hbm, other_ref, index_ref, table_ref, echo_ref, done):
    gates = echo_hbm.shape[3]
    width = gates // ECHO_STEPS
    small = [
        pltpu.make_async_copy(index_hbm, index_ref, done.at[ECHO_STEPS]),
        pltpu.make_async_copy(table_hbm, table_ref, done.at[ECHO_STEPS + 1]),
    ]
    spans = [slice(step * width, (step + 1) * width) for step in range(ECHO_STEPS)]
    large = [
        pltpu.make_async_copy(echo_hbm.at[:, :, :, span], echo_ref.at[:, :, :, span], done.at[step])
        for step, span in enumerate(spans)
    ]
    for copy in small + large:
        copy.start()
    for copy in small:
        copy.wait()
    weights = steering(table_ref, index_ref, other_ref.shape[0], 1 - lax.axis_index("c"))
    for span, copy in zip(spans, large):
        copy.wait()
        other_ref[:, span] = beam_chunk(weights, echo_ref, span)


def own_kernel(index_ref, table_ref, echo_ref, own_ref):
    gates = own_ref.shape[1]
    width = gates // ECHO_STEPS
    weights = steering(table_ref, index_ref, own_ref.shape[0], lax.axis_index("c"))
    for step in range(ECHO_STEPS):
        span = slice(step * width, (step + 1) * width)
        own_ref[:, span] = beam_chunk(weights, echo_ref, span)


def beamform(echoes, steer_table, beam_index):
    _, _, pulses, gates = echoes.shape
    beams = beam_index.shape[0]
    partial = jax.ShapeDtypeStruct((beams * pulses, gates), bf16)
    operands = (beam_index.reshape(1, beams), steer_table, echoes)
    near = pl.BlockSpec(memory_space=pltpu.VMEM)
    other, *held = pl.pallas_call(
        other_kernel,
        in_specs=[pl.BlockSpec(memory_space=pltpu.HBM)] * 3,
        out_specs=[near] * 4,
        out_shape=[partial] + [jax.ShapeDtypeStruct(a.shape, a.dtype) for a in operands],
        scratch_shapes=[pltpu.SemaphoreType.DMA((ECHO_STEPS + 2,))],
        compiler_params=pltpu.CompilerParams(vmem_limit_bytes=VMEM_BYTES),
    )(*(pltpu.with_memory_space_constraint(a, pltpu.HBM) for a in operands))

    def own():
        return pl.pallas_call(
            own_kernel,
            in_specs=[near] * 3,
            out_specs=near,
            out_shape=partial,
            compiler_params=pltpu.CompilerParams(vmem_limit_bytes=VMEM_BYTES),
            cost_estimate=pl.CostEstimate(flops=1 << 30, bytes_accessed=1 << 22, transcendentals=0),
        )(*held)

    return other, own


def band_kernel(code_ref, band_ref):
    taps = code_ref.shape[1]
    for part in range(2):
        code = code_ref[part : part + 1, :].astype(f32)
        code = jnp.concatenate([code, jnp.zeros_like(code)], 1)
        code = jnp.broadcast_to(code, (taps, 2 * taps))
        band_ref[part] = pltpu.roll(code, 0, 1, stride=1, stride_axis=0).astype(bf16)


def toeplitz_bands(pulse_code):
    taps = pulse_code.shape[1]
    return pl.pallas_call(
        band_kernel,
        out_shape=jax.ShapeDtypeStruct((2, taps, 2 * taps), bf16),
        compiler_params=pltpu.CompilerParams(vmem_limit_bytes=VMEM_BYTES),
        cost_estimate=pl.CostEstimate(flops=1 << 22, bytes_accessed=1 << 22, transcendentals=0),
    )(pulse_code)


def add_kernel(own_ref, came_ref, out_ref):
    rows = out_ref.shape[1]
    for chunk in range(out_ref.shape[0]):
        here = slice(chunk * rows, (chunk + 1) * rows)
        out_ref[chunk] = (own_ref[here].astype(f32) + came_ref[here].astype(f32)).astype(bf16)


def added(own, came, chunks):
    rows, gates = own.shape
    return pl.pallas_call(
        add_kernel,
        out_shape=jax.ShapeDtypeStruct((chunks, rows // chunks, gates), bf16),
        compiler_params=pltpu.CompilerParams(vmem_limit_bytes=VMEM_BYTES),
    )(own, came)


def compress_kernel(parts_ref, band_ref, out_ref):
    sources, rows, _ = parts_ref.shape
    chips, slabs = out_ref.shape[:2]
    taps = band_ref.shape[1]
    signal = parts_ref[0].astype(f32)
    for source in range(1, sources):
        signal += parts_ref[source].astype(f32)
    imag = lax.rem(iota(signal.shape, 0), 2) == 1
    turned = jnp.where(imag, -pltpu.roll(signal, 1, 0), pltpu.roll(signal, rows - 1, 0))
    past = jnp.zeros((rows, taps), bf16)
    total = None
    for part, values in enumerate((signal, turned)):
        values = jnp.concatenate([values.astype(bf16), past], 1)
        windows = [values[:, slab * taps : (slab + 2) * taps] for slab in range(slabs)]
        windows = jnp.concatenate(windows, 0)
        product = lax.dot_general(windows, band_ref[part], LAST, preferred_element_type=f32)
        total = product if total is None else total + product
    total = total.reshape(slabs, chips, PAIR, taps)
    for slab in range(slabs):
        block = total[slab]
        out_ref[:, slab] = jnp.concatenate([block[:, :, :LANES], block[:, :, LANES:]], 1).astype(bf16)


def compress(parts, bands):
    _, rows, gates = parts.shape
    taps = bands.shape[1]
    return pl.pallas_call(
        compress_kernel,
        out_shape=jax.ShapeDtypeStruct((rows // PAIR, gates // taps, 2 * PAIR, LANES), bf16),
        compiler_params=pltpu.CompilerParams(vmem_limit_bytes=VMEM_BYTES),
    )(parts, bands)


def delays(value, spacing):
    rows, width = value.shape
    planes = PAIR // 2
    zeros = jnp.zeros((PAIR, width), f32)
    padded = jnp.concatenate([zeros, zeros, zeros, value], 0)
    turned = pltpu.roll(padded, planes, 0)

    def late(pulses):
        source, first = (padded, 3 * PAIR - pulses * planes) if pulses % 2 == 0 else (turned, 3 * PAIR - (pulses - 1) * planes)
        return source[first : first + rows]

    near = jnp.where(spacing == 1, late(1), jnp.where(spacing == 2, late(2), late(3)))
    far = jnp.where(spacing == 1, late(2), jnp.where(spacing == 2, late(4), late(6)))
    return near, far


def filter_kernel(taps_ref, dilation_ref, parts_ref, out_ref, value_ref):
    count, pairs = parts_ref.shape[:2]
    planes, pulses = out_ref.shape[:2]
    rows = pairs * PAIR
    for side in range(2):
        here = slice(side * PAIR, (side + 1) * PAIR)
        total = parts_ref[0, :, here].astype(f32)
        for source in range(1, count):
            total += parts_ref[source, :, here].astype(f32)
        value = total.reshape(rows, LANES)
        for section in range(2):
            spacing = jnp.broadcast_to(dilation_ref[:, section : section + 1], value.shape)
            near, far = delays(value, spacing)
            value = value - taps_ref[section : section + 1, 0:1] * near - taps_ref[section : section + 1, 1:2] * far
        value_ref[...] = value
        for plane in range(planes):
            out_ref[plane, :, side * LANES : (side + 1) * LANES] = value_ref[pl.ds(plane, pulses, stride=planes), :]


def clutter_filter(parts, clutter_taps, dilation):
    pulses = 2 * parts.shape[1]
    planes = PAIR // 2
    near = pl.BlockSpec(memory_space=pltpu.VMEM)
    return pl.pallas_call(
        filter_kernel,
        in_specs=[near] * 3,
        out_shape=jax.ShapeDtypeStruct((planes, pulses, 2 * LANES), f32),
        scratch_shapes=[pltpu.VMEM((pulses * planes, LANES), f32)],
        compiler_params=pltpu.CompilerParams(vmem_limit_bytes=VMEM_BYTES),
    )(clutter_taps, dilation.reshape(1, -1), parts)


def on_device(echoes, steer_table, beam_index, pulse_code, clutter_taps, dilation):
    x_count, z_count = lax.axis_size("x"), lax.axis_size("z")
    slabs = lax.axis_size("y") * lax.axis_size("w")
    other, own = beamform(echoes, steer_table, beam_index)
    came = lax.ppermute(other, "c", [(0, 1), (1, 0)])
    own = own()
    bands = toeplitz_bands(pulse_code)
    came, bands = lax.optimization_barrier((came, bands))
    parts = lax.all_to_all(added(own, came, x_count), "x", 0, 0)
    blocks = compress(parts, bands).reshape(z_count * slabs, 2 * PAIR, LANES)
    blocks = lax.all_to_all(blocks, ("z", "y", "w"), 0, 0)
    blocks = blocks.reshape(z_count, slabs, 2 * PAIR, LANES)
    planes = clutter_filter(blocks, clutter_taps, dilation)
    return planes.reshape(2, 2, planes.shape[1], planes.shape[2])


def solution(mesh):
    split = Mesh(mesh.devices.reshape(4, 4, 2, 8, 2), ("x", "z", "c", "y", "w"))
    elem, gates = ("x", "z", "c"), ("y", "w")
    return jax.shard_map(
        on_device,
        mesh=split,
        in_specs=(P(None, elem, gates, None), P(None, None, elem), P(), P(), P(), P()),
        out_specs=P(elem, None, None, gates),
        check_vma=False,
    )
```

```python
import jax
import jax.numpy as jnp
from jax import lax
from jax.experimental import pallas as pl
from jax.experimental.pallas import tpu as pltpu
from jax.sharding import Mesh, PartitionSpec as P

bf16, f32, i32 = jnp.bfloat16, jnp.float32, jnp.int32
LANES = 128
PAIR = 8
VMEM_BYTES = 24 << 20
ECHO_STEPS = 2
FIRST = (((0,), (0,)), ((), ()))
LAST = (((1,), (1,)), ((), ()))


def iota(shape, dim):
    return lax.broadcasted_iota(i32, shape, dim)


def one_hot(condition):
    return condition.astype(f32).astype(bf16)


def steering(table_ref, index_ref, rows, core):
    elems = table_ref.shape[2]
    beams = index_ref.shape[1]
    select = one_hot(index_ref[...] == iota((table_ref.shape[1], beams), 0))
    row = iota((rows, beams), 0)
    beam = lax.div(row, PAIR) * 4 + core * 2 + lax.rem(lax.div(row, 2), 2)
    pick = one_hot(beam == iota((rows, beams), 1))
    parts = []
    for part in range(2):
        chosen = lax.dot_general(select, table_ref[part], FIRST, preferred_element_type=f32)
        parts.append(jnp.dot(pick, chosen.astype(bf16), preferred_element_type=f32))
    imag = lax.rem(iota((rows, elems), 0), 2) == 1
    by_real = jnp.where(imag, parts[1], parts[0]).astype(bf16)
    by_imag = jnp.where(imag, parts[0], -parts[1]).astype(bf16)
    widen = one_hot(lax.div(iota((elems, 2 * elems), 1), 2) == iota((elems, 2 * elems), 0))
    same_pulse = lax.div(lax.rem(iota((rows, 2 * elems), 0), PAIR), 4) == lax.rem(iota((rows, 2 * elems), 1), 2)
    wide = [
        jnp.where(same_pulse, jnp.dot(m, widen, preferred_element_type=f32), 0.0).astype(bf16)
        for m in (by_real, by_imag)
    ]
    return jnp.concatenate(wide, 1)


def beam_chunk(weights, echo_ref, span):
    samples = echo_ref[:, :, :, span].reshape(weights.shape[1], -1)
    return jnp.dot(weights, samples, preferred_element_type=f32).astype(bf16)


def other_kernel(index_hbm, table_hbm, echo_hbm, other_ref, index_ref, table_ref, echo_ref, done):
    parts, elems, pulses, gates = echo_hbm.shape
    width = gates // ECHO_STEPS
    pieces = [(step * width, part) for step in range(ECHO_STEPS) for part in range(parts)]
    small = [
        pltpu.make_async_copy(index_hbm, index_ref, done.at[len(pieces)]),
        pltpu.make_async_copy(table_hbm, table_ref, done.at[len(pieces) + 1]),
    ]
    large = [
        pltpu.make_async_copy(
            echo_hbm.at[part, :, :, first : first + width], echo_ref.at[part, :, :, first : first + width], done.at[i]
        )
        for i, (first, part) in enumerate(pieces)
    ]
    for copy in small + large:
        copy.start()
    for copy in small:
        copy.wait()
    weights = steering(table_ref, index_ref, other_ref.shape[0], 1 - lax.axis_index("c"))
    depth = elems * pulses
    total = None
    for (first, part), copy in zip(pieces, large):
        copy.wait()
        samples = echo_ref[part, :, :, first : first + width].reshape(depth, width)
        term = jnp.dot(weights[:, part * depth : (part + 1) * depth], samples, preferred_element_type=f32)
        total = term if part == 0 else total + term
        if part == parts - 1:
            other_ref[:, first : first + width] = total.astype(bf16)


def own_kernel(index_ref, table_ref, echo_ref, own_ref):
    gates = own_ref.shape[1]
    width = gates // ECHO_STEPS
    weights = steering(table_ref, index_ref, own_ref.shape[0], lax.axis_index("c"))
    for step in range(ECHO_STEPS):
        span = slice(step * width, (step + 1) * width)
        own_ref[:, span] = beam_chunk(weights, echo_ref, span)


def beamform(echoes, steer_table, beam_index):
    _, _, pulses, gates = echoes.shape
    beams = beam_index.shape[0]
    partial = jax.ShapeDtypeStruct((beams * pulses, gates), bf16)
    operands = (beam_index.reshape(1, beams), steer_table, echoes)
    near = pl.BlockSpec(memory_space=pltpu.VMEM)
    other, *held = pl.pallas_call(
        other_kernel,
        in_specs=[pl.BlockSpec(memory_space=pltpu.HBM)] * 3,
        out_specs=[near] * 4,
        out_shape=[partial] + [jax.ShapeDtypeStruct(a.shape, a.dtype) for a in operands],
        scratch_shapes=[pltpu.SemaphoreType.DMA((2 * ECHO_STEPS + 2,))],
        compiler_params=pltpu.CompilerParams(vmem_limit_bytes=VMEM_BYTES),
    )(*(pltpu.with_memory_space_constraint(a, pltpu.HBM) for a in operands))

    def own():
        return pl.pallas_call(
            own_kernel,
            in_specs=[near] * 3,
            out_specs=near,
            out_shape=partial,
            compiler_params=pltpu.CompilerParams(vmem_limit_bytes=VMEM_BYTES),
            cost_estimate=pl.CostEstimate(flops=1 << 30, bytes_accessed=1 << 22, transcendentals=0),
        )(*held)

    return other, own


def band_kernel(code_ref, band_ref):
    taps = code_ref.shape[1]
    for part in range(2):
        code = code_ref[part : part + 1, :].astype(f32)
        code = jnp.concatenate([code, jnp.zeros_like(code)], 1)
        code = jnp.broadcast_to(code, (taps, 2 * taps))
        band_ref[part] = pltpu.roll(code, 0, 1, stride=1, stride_axis=0).astype(bf16)


def toeplitz_bands(pulse_code):
    taps = pulse_code.shape[1]
    return pl.pallas_call(
        band_kernel,
        out_shape=jax.ShapeDtypeStruct((2, taps, 2 * taps), bf16),
        compiler_params=pltpu.CompilerParams(vmem_limit_bytes=VMEM_BYTES),
        cost_estimate=pl.CostEstimate(flops=1 << 22, bytes_accessed=1 << 22, transcendentals=0),
    )(pulse_code)


def add_kernel(own_ref, came_ref, out_ref):
    rows = out_ref.shape[1]
    for chunk in range(out_ref.shape[0]):
        here = slice(chunk * rows, (chunk + 1) * rows)
        out_ref[chunk] = (own_ref[here].astype(f32) + came_ref[here].astype(f32)).astype(bf16)


def added(own, came, chunks):
    rows, gates = own.shape
    return pl.pallas_call(
        add_kernel,
        out_shape=jax.ShapeDtypeStruct((chunks, rows // chunks, gates), bf16),
        compiler_params=pltpu.CompilerParams(vmem_limit_bytes=VMEM_BYTES),
    )(own, came)


def compress_kernel(parts_ref, band_ref, out_ref):
    sources, rows, _ = parts_ref.shape
    chips, slabs = out_ref.shape[:2]
    taps = band_ref.shape[1]
    signal = parts_ref[0].astype(f32)
    for source in range(1, sources):
        signal += parts_ref[source].astype(f32)
    imag = lax.rem(iota(signal.shape, 0), 2) == 1
    turned = jnp.where(imag, -pltpu.roll(signal, 1, 0), pltpu.roll(signal, rows - 1, 0))
    past = jnp.zeros((rows, taps), bf16)
    total = None
    for part, values in enumerate((signal, turned)):
        values = jnp.concatenate([values.astype(bf16), past], 1)
        windows = [values[:, slab * taps : (slab + 2) * taps] for slab in range(slabs)]
        windows = jnp.concatenate(windows, 0)
        product = lax.dot_general(windows, band_ref[part], LAST, preferred_element_type=f32)
        total = product if total is None else total + product
    total = total.reshape(slabs, chips, PAIR, taps)
    for slab in range(slabs):
        block = total[slab]
        out_ref[:, slab] = jnp.concatenate([block[:, :, :LANES], block[:, :, LANES:]], 1).astype(bf16)


def compress(parts, bands):
    _, rows, gates = parts.shape
    taps = bands.shape[1]
    return pl.pallas_call(
        compress_kernel,
        out_shape=jax.ShapeDtypeStruct((rows // PAIR, gates // taps, 2 * PAIR, LANES), bf16),
        compiler_params=pltpu.CompilerParams(vmem_limit_bytes=VMEM_BYTES),
    )(parts, bands)


def delays(value, spacing):
    rows, width = value.shape
    planes = PAIR // 2
    zeros = jnp.zeros((PAIR, width), f32)
    padded = jnp.concatenate([zeros, zeros, zeros, value], 0)
    turned = pltpu.roll(padded, planes, 0)

    def late(pulses):
        source, first = (padded, 3 * PAIR - pulses * planes) if pulses % 2 == 0 else (turned, 3 * PAIR - (pulses - 1) * planes)
        return source[first : first + rows]

    near = jnp.where(spacing == 1, late(1), jnp.where(spacing == 2, late(2), late(3)))
    far = jnp.where(spacing == 1, late(2), jnp.where(spacing == 2, late(4), late(6)))
    return near, far


def filter_kernel(taps_ref, dilation_ref, parts_ref, out_ref, value_ref):
    count, pairs = parts_ref.shape[:2]
    planes, pulses = out_ref.shape[:2]
    rows = pairs * PAIR
    for side in range(2):
        here = slice(side * PAIR, (side + 1) * PAIR)
        total = parts_ref[0, :, here].astype(f32)
        for source in range(1, count):
            total += parts_ref[source, :, here].astype(f32)
        value = total.reshape(rows, LANES)
        for section in range(2):
            spacing = jnp.broadcast_to(dilation_ref[:, section : section + 1], value.shape)
            near, far = delays(value, spacing)
            value = value - taps_ref[section : section + 1, 0:1] * near - taps_ref[section : section + 1, 1:2] * far
        value_ref[...] = value
        for plane in range(planes):
            out_ref[plane, :, side * LANES : (side + 1) * LANES] = value_ref[pl.ds(plane, pulses, stride=planes), :]


def clutter_filter(parts, clutter_taps, dilation):
    pulses = 2 * parts.shape[1]
    planes = PAIR // 2
    near = pl.BlockSpec(memory_space=pltpu.VMEM)
    return pl.pallas_call(
        filter_kernel,
        in_specs=[near] * 3,
        out_shape=jax.ShapeDtypeStruct((planes, pulses, 2 * LANES), f32),
        scratch_shapes=[pltpu.VMEM((pulses * planes, LANES), f32)],
        compiler_params=pltpu.CompilerParams(vmem_limit_bytes=VMEM_BYTES),
    )(clutter_taps, dilation.reshape(1, -1), parts)


def on_device(echoes, steer_table, beam_index, pulse_code, clutter_taps, dilation):
    x_count, z_count = lax.axis_size("x"), lax.axis_size("z")
    slabs = lax.axis_size("y") * lax.axis_size("w")
    other, own = beamform(echoes, steer_table, beam_index)
    came = lax.ppermute(other, "c", [(0, 1), (1, 0)])
    own = own()
    bands = toeplitz_bands(pulse_code)
    came, bands = lax.optimization_barrier((came, bands))
    parts = lax.all_to_all(added(own, came, x_count), "x", 0, 0)
    blocks = compress(parts, bands).reshape(z_count * slabs, 2 * PAIR, LANES)
    blocks = lax.all_to_all(blocks, ("z", "y", "w"), 0, 0)
    blocks = blocks.reshape(z_count, slabs, 2 * PAIR, LANES)
    planes = clutter_filter(blocks, clutter_taps, dilation)
    return planes.reshape(2, 2, planes.shape[1], planes.shape[2])


def solution(mesh):
    split = Mesh(mesh.devices.reshape(4, 4, 2, 8, 2), ("x", "z", "c", "y", "w"))
    elem, gates = ("x", "z", "c"), ("y", "w")
    return jax.shard_map(
        on_device,
        mesh=split,
        in_specs=(P(None, elem, gates, None), P(None, None, elem), P(), P(), P(), P()),
        out_specs=P(elem, None, None, gates),
        check_vma=False,
    )
```

```python
import jax
import jax.numpy as jnp
from jax import lax
from jax.experimental import pallas as pl
from jax.experimental.pallas import tpu as pltpu
from jax.sharding import Mesh, PartitionSpec as P

bf16, f32, i32 = jnp.bfloat16, jnp.float32, jnp.int32
LANES = 128
PAIR = 8
VMEM_BYTES = 24 << 20
ECHO_STEPS = 2
FIRST = (((0,), (0,)), ((), ()))
LAST = (((1,), (1,)), ((), ()))


def iota(shape, dim):
    return lax.broadcasted_iota(i32, shape, dim)


def one_hot(condition):
    return condition.astype(f32).astype(bf16)


def steering(table_ref, index_ref, rows, core):
    elems = table_ref.shape[2]
    beams = index_ref.shape[1]
    select = one_hot(index_ref[...] == iota((table_ref.shape[1], beams), 0))
    row = iota((rows, beams), 0)
    beam = lax.div(row, PAIR) * 4 + core * 2 + lax.rem(lax.div(row, 2), 2)
    pick = one_hot(beam == iota((rows, beams), 1))
    parts = []
    for part in range(2):
        chosen = lax.dot_general(select, table_ref[part], FIRST, preferred_element_type=f32)
        parts.append(jnp.dot(pick, chosen.astype(bf16), preferred_element_type=f32))
    imag = lax.rem(iota((rows, elems), 0), 2) == 1
    by_real = jnp.where(imag, parts[1], parts[0]).astype(bf16)
    by_imag = jnp.where(imag, parts[0], -parts[1]).astype(bf16)
    widen = one_hot(lax.div(iota((elems, 2 * elems), 1), 2) == iota((elems, 2 * elems), 0))
    same_pulse = lax.div(lax.rem(iota((rows, 2 * elems), 0), PAIR), 4) == lax.rem(iota((rows, 2 * elems), 1), 2)
    wide = [
        jnp.where(same_pulse, jnp.dot(m, widen, preferred_element_type=f32), 0.0).astype(bf16)
        for m in (by_real, by_imag)
    ]
    return jnp.concatenate(wide, 1)


def beam_chunk(weights, echo_ref, span):
    samples = echo_ref[:, :, :, span].reshape(weights.shape[1], -1)
    return jnp.dot(weights, samples, preferred_element_type=f32).astype(bf16)


def other_kernel(index_hbm, table_hbm, echo_hbm, other_ref, index_ref, table_ref, echo_ref, done):
    parts, elems, pulses, gates = echo_hbm.shape
    width = gates // ECHO_STEPS
    pieces = [(step * width, part) for step in range(ECHO_STEPS) for part in range(parts)]
    small = [
        pltpu.make_async_copy(index_hbm, index_ref, done.at[len(pieces)]),
        pltpu.make_async_copy(table_hbm, table_ref, done.at[len(pieces) + 1]),
    ]
    large = [
        pltpu.make_async_copy(
            echo_hbm.at[part, :, :, first : first + width], echo_ref.at[part, :, :, first : first + width], done.at[i]
        )
        for i, (first, part) in enumerate(pieces)
    ]
    for copy in small + large:
        copy.start()
    for copy in small:
        copy.wait()
    weights = steering(table_ref, index_ref, other_ref.shape[0], 1 - lax.axis_index("c"))
    depth = elems * pulses
    total = None
    for (first, part), copy in zip(pieces, large):
        copy.wait()
        samples = echo_ref[part, :, :, first : first + width].reshape(depth, width)
        term = jnp.dot(weights[:, part * depth : (part + 1) * depth], samples, preferred_element_type=f32)
        total = term if part == 0 else total + term
        if part == parts - 1:
            other_ref[:, first : first + width] = total.astype(bf16)


def own_kernel(index_ref, table_ref, echo_ref, own_ref):
    gates = own_ref.shape[1]
    width = gates // ECHO_STEPS
    weights = steering(table_ref, index_ref, own_ref.shape[0], lax.axis_index("c"))
    for step in range(ECHO_STEPS):
        span = slice(step * width, (step + 1) * width)
        own_ref[:, span] = beam_chunk(weights, echo_ref, span)


def beamform(echoes, steer_table, beam_index):
    _, _, pulses, gates = echoes.shape
    beams = beam_index.shape[0]
    partial = jax.ShapeDtypeStruct((beams * pulses, gates), bf16)
    operands = (beam_index.reshape(1, beams), steer_table, echoes)
    near = pl.BlockSpec(memory_space=pltpu.VMEM)
    other, *held = pl.pallas_call(
        other_kernel,
        in_specs=[pl.BlockSpec(memory_space=pltpu.HBM)] * 3,
        out_specs=[near] * 4,
        out_shape=[partial] + [jax.ShapeDtypeStruct(a.shape, a.dtype) for a in operands],
        scratch_shapes=[pltpu.SemaphoreType.DMA((2 * ECHO_STEPS + 2,))],
        compiler_params=pltpu.CompilerParams(vmem_limit_bytes=VMEM_BYTES),
    )(*(pltpu.with_memory_space_constraint(a, pltpu.HBM) for a in operands))

    def own():
        return pl.pallas_call(
            own_kernel,
            in_specs=[near] * 3,
            out_specs=near,
            out_shape=partial,
            compiler_params=pltpu.CompilerParams(vmem_limit_bytes=VMEM_BYTES),
            cost_estimate=pl.CostEstimate(flops=1 << 30, bytes_accessed=1 << 22, transcendentals=0),
        )(*held)

    return other, own


def band_kernel(code_ref, band_ref):
    taps = code_ref.shape[1]
    for part in range(2):
        code = code_ref[part : part + 1, :].astype(f32)
        code = jnp.concatenate([code, jnp.zeros_like(code)], 1)
        code = jnp.broadcast_to(code, (taps, 2 * taps))
        band_ref[part] = pltpu.roll(code, 0, 1, stride=1, stride_axis=0).astype(bf16)


def toeplitz_bands(pulse_code):
    taps = pulse_code.shape[1]
    return pl.pallas_call(
        band_kernel,
        out_shape=jax.ShapeDtypeStruct((2, taps, 2 * taps), bf16),
        compiler_params=pltpu.CompilerParams(vmem_limit_bytes=VMEM_BYTES),
        cost_estimate=pl.CostEstimate(flops=1 << 22, bytes_accessed=1 << 22, transcendentals=0),
    )(pulse_code)


def add_kernel(own_ref, came_ref, out_ref):
    rows = out_ref.shape[1]
    for chunk in range(out_ref.shape[0]):
        here = slice(chunk * rows, (chunk + 1) * rows)
        out_ref[chunk] = (own_ref[here].astype(f32) + came_ref[here].astype(f32)).astype(bf16)


def added(own, came, chunks):
    rows, gates = own.shape
    return pl.pallas_call(
        add_kernel,
        out_shape=jax.ShapeDtypeStruct((chunks, rows // chunks, gates), bf16),
        compiler_params=pltpu.CompilerParams(vmem_limit_bytes=VMEM_BYTES),
    )(own, came)


def compress_kernel(parts_ref, band_ref, out_ref):
    sources, rows, _ = parts_ref.shape
    chips, slabs = out_ref.shape[:2]
    taps = band_ref.shape[1]
    signal = parts_ref[0].astype(f32)
    for source in range(1, sources):
        signal += parts_ref[source].astype(f32)
    values = jnp.concatenate([signal.astype(bf16), jnp.zeros((rows, taps), bf16)], 1)
    windows = jnp.concatenate([values[:, slab * taps : (slab + 2) * taps] for slab in range(slabs)], 0)
    by_real, by_imag = (
        lax.dot_general(windows, band_ref[part], LAST, preferred_element_type=f32) for part in range(2)
    )
    imag = lax.rem(iota(by_imag.shape, 0), 2) == 1
    total = by_real + jnp.where(imag, -pltpu.roll(by_imag, 1, 0), pltpu.roll(by_imag, rows * slabs - 1, 0))
    total = total.reshape(slabs, chips, PAIR, taps)
    for slab in range(slabs):
        block = total[slab]
        out_ref[:, slab] = jnp.concatenate([block[:, :, :LANES], block[:, :, LANES:]], 1).astype(bf16)


def compress(parts, bands):
    _, rows, gates = parts.shape
    taps = bands.shape[1]
    return pl.pallas_call(
        compress_kernel,
        out_shape=jax.ShapeDtypeStruct((rows // PAIR, gates // taps, 2 * PAIR, LANES), bf16),
        compiler_params=pltpu.CompilerParams(vmem_limit_bytes=VMEM_BYTES),
    )(parts, bands)


def delays(value, spacing):
    rows, width = value.shape
    planes = PAIR // 2
    zeros = jnp.zeros((PAIR, width), f32)
    padded = jnp.concatenate([zeros, zeros, zeros, value], 0)
    turned = pltpu.roll(padded, planes, 0)

    def late(pulses):
        source, first = (padded, 3 * PAIR - pulses * planes) if pulses % 2 == 0 else (turned, 3 * PAIR - (pulses - 1) * planes)
        return source[first : first + rows]

    near = jnp.where(spacing == 1, late(1), jnp.where(spacing == 2, late(2), late(3)))
    far = jnp.where(spacing == 1, late(2), jnp.where(spacing == 2, late(4), late(6)))
    return near, far


def filter_kernel(taps_ref, dilation_ref, parts_ref, out_ref, value_ref):
    count, pairs = parts_ref.shape[:2]
    planes, pulses = out_ref.shape[:2]
    rows = pairs * PAIR
    for side in range(2):
        here = slice(side * PAIR, (side + 1) * PAIR)
        total = parts_ref[0, :, here].astype(f32)
        for source in range(1, count):
            total += parts_ref[source, :, here].astype(f32)
        value = total.reshape(rows, LANES)
        for section in range(2):
            spacing = jnp.broadcast_to(dilation_ref[:, section : section + 1], value.shape)
            near, far = delays(value, spacing)
            value = value - taps_ref[section : section + 1, 0:1] * near - taps_ref[section : section + 1, 1:2] * far
        value_ref[...] = value
        for plane in range(planes):
            out_ref[plane, :, side * LANES : (side + 1) * LANES] = value_ref[pl.ds(plane, pulses, stride=planes), :]


def clutter_filter(parts, clutter_taps, dilation):
    pulses = 2 * parts.shape[1]
    planes = PAIR // 2
    near = pl.BlockSpec(memory_space=pltpu.VMEM)
    return pl.pallas_call(
        filter_kernel,
        in_specs=[near] * 3,
        out_shape=jax.ShapeDtypeStruct((planes, pulses, 2 * LANES), f32),
        scratch_shapes=[pltpu.VMEM((pulses * planes, LANES), f32)],
        compiler_params=pltpu.CompilerParams(vmem_limit_bytes=VMEM_BYTES),
    )(clutter_taps, dilation.reshape(1, -1), parts)


def on_device(echoes, steer_table, beam_index, pulse_code, clutter_taps, dilation):
    x_count, z_count = lax.axis_size("x"), lax.axis_size("z")
    slabs = lax.axis_size("y") * lax.axis_size("w")
    other, own = beamform(echoes, steer_table, beam_index)
    came = lax.ppermute(other, "c", [(0, 1), (1, 0)])
    own = own()
    bands = toeplitz_bands(pulse_code)
    came, bands = lax.optimization_barrier((came, bands))
    parts = lax.all_to_all(added(own, came, x_count), "x", 0, 0)
    blocks = compress(parts, bands).reshape(z_count * slabs, 2 * PAIR, LANES)
    blocks = lax.all_to_all(blocks, ("z", "y", "w"), 0, 0)
    blocks = blocks.reshape(z_count, slabs, 2 * PAIR, LANES)
    planes = clutter_filter(blocks, clutter_taps, dilation)
    return planes.reshape(2, 2, planes.shape[1], planes.shape[2])


def solution(mesh):
    split = Mesh(mesh.devices.reshape(4, 4, 2, 8, 2), ("x", "z", "c", "y", "w"))
    elem, gates = ("x", "z", "c"), ("y", "w")
    return jax.shard_map(
        on_device,
        mesh=split,
        in_specs=(P(None, elem, gates, None), P(None, None, elem), P(), P(), P(), P()),
        out_specs=P(elem, None, None, gates),
        check_vma=False,
    )
```

```python
import jax
import jax.numpy as jnp
from jax import lax
from jax.experimental import pallas as pl
from jax.experimental.pallas import tpu as pltpu
from jax.sharding import Mesh, PartitionSpec as P

bf16, f32, i32 = jnp.bfloat16, jnp.float32, jnp.int32
LANES = 128
PAIR = 8
VMEM_BYTES = 24 << 20
ECHO_STEPS = 2
FIRST = (((0,), (0,)), ((), ()))
LAST = (((1,), (1,)), ((), ()))


def iota(shape, dim):
    return lax.broadcasted_iota(i32, shape, dim)


def one_hot(condition):
    return condition.astype(f32).astype(bf16)


def steering(table_ref, index_ref, rows, core):
    elems = table_ref.shape[2]
    beams = index_ref.shape[1]
    select = one_hot(index_ref[...] == iota((table_ref.shape[1], beams), 0))
    row = iota((rows, beams), 0)
    beam = lax.div(row, PAIR) * 4 + core * 2 + lax.rem(lax.div(row, 2), 2)
    pick = one_hot(beam == iota((rows, beams), 1))
    parts = []
    for part in range(2):
        chosen = lax.dot_general(select, table_ref[part], FIRST, preferred_element_type=f32)
        parts.append(jnp.dot(pick, chosen.astype(bf16), preferred_element_type=f32))
    imag = lax.rem(iota((rows, elems), 0), 2) == 1
    by_real = jnp.where(imag, parts[1], parts[0]).astype(bf16)
    by_imag = jnp.where(imag, parts[0], -parts[1]).astype(bf16)
    widen = one_hot(lax.div(iota((elems, 2 * elems), 1), 2) == iota((elems, 2 * elems), 0))
    same_pulse = lax.div(lax.rem(iota((rows, 2 * elems), 0), PAIR), 4) == lax.rem(iota((rows, 2 * elems), 1), 2)
    wide = [
        jnp.where(same_pulse, jnp.dot(m, widen, preferred_element_type=f32), 0.0).astype(bf16)
        for m in (by_real, by_imag)
    ]
    return jnp.concatenate(wide, 1)


def beam_chunk(weights, echo_ref, span):
    samples = echo_ref[:, :, :, span].reshape(weights.shape[1], -1)
    return jnp.dot(weights, samples, preferred_element_type=f32).astype(bf16)


def other_kernel(index_hbm, table_hbm, echo_hbm, other_ref, index_ref, table_ref, echo_ref, done):
    parts, elems, pulses, gates = echo_hbm.shape
    width = gates // ECHO_STEPS
    pieces = [(step * width, part) for step in range(ECHO_STEPS) for part in range(parts)]
    small = [
        pltpu.make_async_copy(index_hbm, index_ref, done.at[len(pieces)]),
        pltpu.make_async_copy(table_hbm, table_ref, done.at[len(pieces) + 1]),
    ]
    large = [
        pltpu.make_async_copy(
            echo_hbm.at[part, :, :, first : first + width], echo_ref.at[part, :, :, first : first + width], done.at[i]
        )
        for i, (first, part) in enumerate(pieces)
    ]
    for copy in small + large:
        copy.start()
    for copy in small:
        copy.wait()
    weights = steering(table_ref, index_ref, other_ref.shape[0], 1 - lax.axis_index("c"))
    depth = elems * pulses
    total = None
    for (first, part), copy in zip(pieces, large):
        copy.wait()
        samples = echo_ref[part, :, :, first : first + width].reshape(depth, width)
        term = jnp.dot(weights[:, part * depth : (part + 1) * depth], samples, preferred_element_type=f32)
        total = term if part == 0 else total + term
        if part == parts - 1:
            other_ref[:, first : first + width] = total.astype(bf16)


def own_kernel(index_ref, table_ref, echo_ref, own_ref):
    gates = own_ref.shape[1]
    width = gates // ECHO_STEPS
    weights = steering(table_ref, index_ref, own_ref.shape[0], lax.axis_index("c"))
    for step in range(ECHO_STEPS):
        span = slice(step * width, (step + 1) * width)
        own_ref[:, span] = beam_chunk(weights, echo_ref, span)


def beamform(echoes, steer_table, beam_index):
    _, _, pulses, gates = echoes.shape
    beams = beam_index.shape[0]
    partial = jax.ShapeDtypeStruct((beams * pulses, gates), bf16)
    operands = (beam_index.reshape(1, beams), steer_table, echoes)
    near = pl.BlockSpec(memory_space=pltpu.VMEM)
    other, *held = pl.pallas_call(
        other_kernel,
        in_specs=[pl.BlockSpec(memory_space=pltpu.HBM)] * 3,
        out_specs=[near] * 4,
        out_shape=[partial] + [jax.ShapeDtypeStruct(a.shape, a.dtype) for a in operands],
        scratch_shapes=[pltpu.SemaphoreType.DMA((2 * ECHO_STEPS + 2,))],
        compiler_params=pltpu.CompilerParams(vmem_limit_bytes=VMEM_BYTES),
    )(*(pltpu.with_memory_space_constraint(a, pltpu.HBM) for a in operands))

    def own():
        return pl.pallas_call(
            own_kernel,
            in_specs=[near] * 3,
            out_specs=near,
            out_shape=partial,
            compiler_params=pltpu.CompilerParams(vmem_limit_bytes=VMEM_BYTES),
            cost_estimate=pl.CostEstimate(flops=1 << 30, bytes_accessed=1 << 22, transcendentals=0),
        )(*held)

    return other, own


def band_kernel(code_ref, band_ref):
    taps = code_ref.shape[1]
    for part in range(2):
        code = code_ref[part : part + 1, :].astype(f32)
        code = jnp.concatenate([code, jnp.zeros_like(code)], 1)
        code = jnp.broadcast_to(code, (taps, 2 * taps))
        band_ref[part] = pltpu.roll(code, 0, 1, stride=1, stride_axis=0).astype(bf16)


def toeplitz_bands(pulse_code):
    taps = pulse_code.shape[1]
    return pl.pallas_call(
        band_kernel,
        out_shape=jax.ShapeDtypeStruct((2, taps, 2 * taps), bf16),
        compiler_params=pltpu.CompilerParams(vmem_limit_bytes=VMEM_BYTES),
        cost_estimate=pl.CostEstimate(flops=1 << 22, bytes_accessed=1 << 22, transcendentals=0),
    )(pulse_code)


def added(own, came, chunks):
    rows, gates = own.shape
    return (own.astype(f32) + came.astype(f32)).astype(bf16).reshape(chunks, rows // chunks, gates)


def compress_kernel(parts_ref, band_ref, out_ref):
    sources, rows, _ = parts_ref.shape
    chips, slabs = out_ref.shape[:2]
    taps = band_ref.shape[1]
    signal = parts_ref[0].astype(f32)
    for source in range(1, sources):
        signal += parts_ref[source].astype(f32)
    values = jnp.concatenate([signal.astype(bf16), jnp.zeros((rows, taps), bf16)], 1)
    windows = jnp.concatenate([values[:, slab * taps : (slab + 2) * taps] for slab in range(slabs)], 0)
    by_real, by_imag = (
        lax.dot_general(windows, band_ref[part], LAST, preferred_element_type=f32) for part in range(2)
    )
    imag = lax.rem(iota(by_imag.shape, 0), 2) == 1
    total = by_real + jnp.where(imag, -pltpu.roll(by_imag, 1, 0), pltpu.roll(by_imag, rows * slabs - 1, 0))
    total = total.reshape(slabs, chips, PAIR, taps)
    for slab in range(slabs):
        block = total[slab]
        out_ref[:, slab] = jnp.concatenate([block[:, :, :LANES], block[:, :, LANES:]], 1).astype(bf16)


def compress(parts, bands):
    _, rows, gates = parts.shape
    taps = bands.shape[1]
    return pl.pallas_call(
        compress_kernel,
        out_shape=jax.ShapeDtypeStruct((rows // PAIR, gates // taps, 2 * PAIR, LANES), bf16),
        compiler_params=pltpu.CompilerParams(vmem_limit_bytes=VMEM_BYTES),
    )(parts, bands)


def delays(value, spacing):
    rows, width = value.shape
    planes = PAIR // 2
    zeros = jnp.zeros((PAIR, width), f32)
    padded = jnp.concatenate([zeros, zeros, zeros, value], 0)
    turned = pltpu.roll(padded, planes, 0)

    def late(pulses):
        source, first = (padded, 3 * PAIR - pulses * planes) if pulses % 2 == 0 else (turned, 3 * PAIR - (pulses - 1) * planes)
        return source[first : first + rows]

    near = jnp.where(spacing == 1, late(1), jnp.where(spacing == 2, late(2), late(3)))
    far = jnp.where(spacing == 1, late(2), jnp.where(spacing == 2, late(4), late(6)))
    return near, far


def filter_kernel(taps_ref, dilation_ref, parts_ref, out_ref, value_ref):
    count, pairs = parts_ref.shape[:2]
    planes, pulses = out_ref.shape[:2]
    rows = pairs * PAIR
    for side in range(2):
        here = slice(side * PAIR, (side + 1) * PAIR)
        total = parts_ref[0, :, here].astype(f32)
        for source in range(1, count):
            total += parts_ref[source, :, here].astype(f32)
        value = total.reshape(rows, LANES)
        for section in range(2):
            spacing = jnp.broadcast_to(dilation_ref[:, section : section + 1], value.shape)
            near, far = delays(value, spacing)
            value = value - taps_ref[section : section + 1, 0:1] * near - taps_ref[section : section + 1, 1:2] * far
        value_ref[...] = value
        for plane in range(planes):
            out_ref[plane, :, side * LANES : (side + 1) * LANES] = value_ref[pl.ds(plane, pulses, stride=planes), :]


def clutter_filter(parts, clutter_taps, dilation):
    pulses = 2 * parts.shape[1]
    planes = PAIR // 2
    near = pl.BlockSpec(memory_space=pltpu.VMEM)
    return pl.pallas_call(
        filter_kernel,
        in_specs=[near] * 3,
        out_shape=jax.ShapeDtypeStruct((planes, pulses, 2 * LANES), f32),
        scratch_shapes=[pltpu.VMEM((pulses * planes, LANES), f32)],
        compiler_params=pltpu.CompilerParams(vmem_limit_bytes=VMEM_BYTES),
    )(clutter_taps, dilation.reshape(1, -1), parts)


def on_device(echoes, steer_table, beam_index, pulse_code, clutter_taps, dilation):
    x_count, z_count = lax.axis_size("x"), lax.axis_size("z")
    slabs = lax.axis_size("y") * lax.axis_size("w")
    other, own = beamform(echoes, steer_table, beam_index)
    came = lax.ppermute(other, "c", [(0, 1), (1, 0)])
    own = own()
    bands = toeplitz_bands(pulse_code)
    came, bands = lax.optimization_barrier((came, bands))
    parts = lax.all_to_all(added(own, came, x_count), "x", 0, 0)
    blocks = compress(parts, bands).reshape(z_count * slabs, 2 * PAIR, LANES)
    blocks = lax.all_to_all(blocks, ("z", "y", "w"), 0, 0)
    blocks = blocks.reshape(z_count, slabs, 2 * PAIR, LANES)
    planes = clutter_filter(blocks, clutter_taps, dilation)
    return planes.reshape(2, 2, planes.shape[1], planes.shape[2])


def solution(mesh):
    split = Mesh(mesh.devices.reshape(4, 4, 2, 8, 2), ("x", "z", "c", "y", "w"))
    elem, gates = ("x", "z", "c"), ("y", "w")
    return jax.shard_map(
        on_device,
        mesh=split,
        in_specs=(P(None, elem, gates, None), P(None, None, elem), P(), P(), P(), P()),
        out_specs=P(elem, None, None, gates),
        check_vma=False,
    )
```

```python
import jax
import jax.numpy as jnp
from jax import lax
from jax.experimental import pallas as pl
from jax.experimental.pallas import tpu as pltpu
from jax.sharding import Mesh, PartitionSpec as P

bf16, f32, i32 = jnp.bfloat16, jnp.float32, jnp.int32
LANES = 128
PAIR = 8
VMEM_BYTES = 24 << 20
ECHO_STEPS = 2
FIRST = (((0,), (0,)), ((), ()))
LAST = (((1,), (1,)), ((), ()))


def iota(shape, dim):
    return lax.broadcasted_iota(i32, shape, dim)


def one_hot(condition):
    return condition.astype(f32).astype(bf16)


def steering(table_ref, index_ref, rows, core):
    elems = table_ref.shape[2]
    beams = index_ref.shape[1]
    select = one_hot(index_ref[...] == iota((table_ref.shape[1], beams), 0))
    row = iota((rows, beams), 0)
    beam = lax.div(row, PAIR) * 4 + core * 2 + lax.rem(lax.div(row, 2), 2)
    pick = one_hot(beam == iota((rows, beams), 1))
    parts = []
    for part in range(2):
        chosen = lax.dot_general(select, table_ref[part], FIRST, preferred_element_type=f32)
        parts.append(jnp.dot(pick, chosen.astype(bf16), preferred_element_type=f32))
    imag = lax.rem(iota((rows, elems), 0), 2) == 1
    by_real = jnp.where(imag, parts[1], parts[0]).astype(bf16)
    by_imag = jnp.where(imag, parts[0], -parts[1]).astype(bf16)
    widen = one_hot(lax.div(iota((elems, 2 * elems), 1), 2) == iota((elems, 2 * elems), 0))
    same_pulse = lax.div(lax.rem(iota((rows, 2 * elems), 0), PAIR), 4) == lax.rem(iota((rows, 2 * elems), 1), 2)
    wide = [
        jnp.where(same_pulse, jnp.dot(m, widen, preferred_element_type=f32), 0.0).astype(bf16)
        for m in (by_real, by_imag)
    ]
    return jnp.concatenate(wide, 1)


def beam_chunk(weights, echo_ref, span):
    samples = echo_ref[:, :, :, span].reshape(weights.shape[1], -1)
    return jnp.dot(weights, samples, preferred_element_type=f32).astype(bf16)


def other_kernel(index_hbm, table_hbm, echo_hbm, other_ref, index_ref, table_ref, echo_ref, done):
    parts, elems, pulses, gates = echo_hbm.shape
    width = gates // ECHO_STEPS
    pieces = [(step * width, part) for step in range(ECHO_STEPS) for part in range(parts)]
    small = [
        pltpu.make_async_copy(index_hbm, index_ref, done.at[len(pieces)]),
        pltpu.make_async_copy(table_hbm, table_ref, done.at[len(pieces) + 1]),
    ]
    large = [
        pltpu.make_async_copy(
            echo_hbm.at[part, :, :, first : first + width], echo_ref.at[part, :, :, first : first + width], done.at[i]
        )
        for i, (first, part) in enumerate(pieces)
    ]
    for copy in small + large:
        copy.start()
    for copy in small:
        copy.wait()
    weights = steering(table_ref, index_ref, other_ref.shape[0], 1 - lax.axis_index("c"))
    depth = elems * pulses
    total = None
    for (first, part), copy in zip(pieces, large):
        copy.wait()
        samples = echo_ref[part, :, :, first : first + width].reshape(depth, width)
        term = jnp.dot(weights[:, part * depth : (part + 1) * depth], samples, preferred_element_type=f32)
        total = term if part == 0 else total + term
        if part == parts - 1:
            other_ref[:, first : first + width] = total.astype(bf16)


def own_kernel(index_ref, table_ref, echo_ref, own_ref):
    gates = own_ref.shape[1]
    width = gates // ECHO_STEPS
    weights = steering(table_ref, index_ref, own_ref.shape[0], lax.axis_index("c"))
    for step in range(ECHO_STEPS):
        span = slice(step * width, (step + 1) * width)
        own_ref[:, span] = beam_chunk(weights, echo_ref, span)


def beamform(echoes, steer_table, beam_index):
    _, _, pulses, gates = echoes.shape
    beams = beam_index.shape[0]
    partial = jax.ShapeDtypeStruct((beams * pulses, gates), bf16)
    operands = (beam_index.reshape(1, beams), steer_table, echoes)
    near = pl.BlockSpec(memory_space=pltpu.VMEM)
    other, *held = pl.pallas_call(
        other_kernel,
        in_specs=[pl.BlockSpec(memory_space=pltpu.HBM)] * 3,
        out_specs=[near] * 4,
        out_shape=[partial] + [jax.ShapeDtypeStruct(a.shape, a.dtype) for a in operands],
        scratch_shapes=[pltpu.SemaphoreType.DMA((2 * ECHO_STEPS + 2,))],
        compiler_params=pltpu.CompilerParams(vmem_limit_bytes=VMEM_BYTES),
    )(*(pltpu.with_memory_space_constraint(a, pltpu.HBM) for a in operands))

    def own():
        return pl.pallas_call(
            own_kernel,
            in_specs=[near] * 3,
            out_specs=near,
            out_shape=partial,
            compiler_params=pltpu.CompilerParams(vmem_limit_bytes=VMEM_BYTES),
            cost_estimate=pl.CostEstimate(flops=1 << 30, bytes_accessed=1 << 22, transcendentals=0),
        )(*held)

    return other, own


def band_kernel(code_ref, band_ref):
    taps = code_ref.shape[1]
    for part in range(2):
        code = code_ref[part : part + 1, :].astype(f32)
        code = jnp.concatenate([code, jnp.zeros_like(code)], 1)
        code = jnp.broadcast_to(code, (taps, 2 * taps))
        band_ref[part] = pltpu.roll(code, 0, 1, stride=1, stride_axis=0).astype(bf16)


def toeplitz_bands(pulse_code):
    taps = pulse_code.shape[1]
    return pl.pallas_call(
        band_kernel,
        out_shape=jax.ShapeDtypeStruct((2, taps, 2 * taps), bf16),
        compiler_params=pltpu.CompilerParams(vmem_limit_bytes=VMEM_BYTES),
        cost_estimate=pl.CostEstimate(flops=1 << 22, bytes_accessed=1 << 22, transcendentals=0),
    )(pulse_code)


def added(own, came, chunks):
    rows, gates = own.shape
    return (own.astype(f32) + came.astype(f32)).astype(bf16).reshape(chunks, rows // chunks, gates)


def compress_kernel(parts_ref, band_ref, out_ref):
    sources, rows, _ = parts_ref.shape
    chips, slabs = out_ref.shape[:2]
    taps = band_ref.shape[1]
    signal = parts_ref[0].astype(f32)
    for source in range(1, sources):
        signal += parts_ref[source].astype(f32)
    values = jnp.concatenate([signal.astype(bf16), jnp.zeros((rows, taps), bf16)], 1)
    windows = jnp.concatenate([values[:, slab * taps : (slab + 2) * taps] for slab in range(slabs)], 0)
    by_real, by_imag = (
        lax.dot_general(windows, band_ref[part], LAST, preferred_element_type=f32) for part in range(2)
    )
    imag = lax.rem(iota(by_imag.shape, 0), 2) == 1
    total = by_real + jnp.where(imag, -pltpu.roll(by_imag, 1, 0), pltpu.roll(by_imag, rows * slabs - 1, 0))
    total = total.reshape(slabs, chips, PAIR, taps)
    for slab in range(slabs):
        block = total[slab]
        out_ref[:, slab] = jnp.concatenate([block[:, :, :LANES], block[:, :, LANES:]], 1).astype(bf16)


def compress(parts, bands):
    _, rows, gates = parts.shape
    taps = bands.shape[1]
    return pl.pallas_call(
        compress_kernel,
        out_shape=jax.ShapeDtypeStruct((rows // PAIR, gates // taps, 2 * PAIR, LANES), bf16),
        compiler_params=pltpu.CompilerParams(vmem_limit_bytes=VMEM_BYTES),
    )(parts, bands)


def delays(value, spacing):
    rows, width = value.shape
    planes = PAIR // 2
    zeros = jnp.zeros((PAIR, width), f32)
    padded = jnp.concatenate([zeros, zeros, zeros, value], 0)
    turned = pltpu.roll(padded, planes, 0)

    def late(pulses):
        source, first = (padded, 3 * PAIR - pulses * planes) if pulses % 2 == 0 else (turned, 3 * PAIR - (pulses - 1) * planes)
        return source[first : first + rows]

    near = jnp.where(spacing == 1, late(1), jnp.where(spacing == 2, late(2), late(3)))
    far = jnp.where(spacing == 1, late(2), jnp.where(spacing == 2, late(4), late(6)))
    return near, far


def filter_kernel(taps_ref, dilation_ref, parts_ref, out_ref, value_ref, side_ref, done):
    count, pairs = parts_ref.shape[:2]
    planes, pulses = out_ref.shape[:2]
    rows = pairs * PAIR
    copies = []
    for side in range(2):
        here = slice(side * PAIR, (side + 1) * PAIR)
        total = parts_ref[0, :, here].astype(f32)
        for source in range(1, count):
            total += parts_ref[source, :, here].astype(f32)
        value = total.reshape(rows, LANES)
        for section in range(2):
            spacing = jnp.broadcast_to(dilation_ref[:, section : section + 1], value.shape)
            near, far = delays(value, spacing)
            value = value - taps_ref[section : section + 1, 0:1] * near - taps_ref[section : section + 1, 1:2] * far
        value_ref[...] = value
        for plane in range(planes):
            side_ref[side, plane] = value_ref[pl.ds(plane, pulses, stride=planes), :]
        lanes = slice(side * LANES, (side + 1) * LANES)
        copies.append(pltpu.make_async_copy(side_ref.at[side], out_ref.at[:, :, lanes], done.at[side]))
        copies[side].start()
    for copy in copies:
        copy.wait()


def clutter_filter(parts, clutter_taps, dilation):
    pulses = 2 * parts.shape[1]
    planes = PAIR // 2
    near = pl.BlockSpec(memory_space=pltpu.VMEM)
    return pl.pallas_call(
        filter_kernel,
        in_specs=[near] * 3,
        out_specs=pl.BlockSpec(memory_space=pltpu.HBM),
        out_shape=jax.ShapeDtypeStruct((planes, pulses, 2 * LANES), f32),
        scratch_shapes=[pltpu.VMEM((pulses * planes, LANES), f32), pltpu.VMEM((2, planes, pulses, LANES), f32), pltpu.SemaphoreType.DMA((2,))],
        compiler_params=pltpu.CompilerParams(vmem_limit_bytes=VMEM_BYTES),
    )(clutter_taps, dilation.reshape(1, -1), parts)


def on_device(echoes, steer_table, beam_index, pulse_code, clutter_taps, dilation):
    x_count, z_count = lax.axis_size("x"), lax.axis_size("z")
    slabs = lax.axis_size("y") * lax.axis_size("w")
    other, own = beamform(echoes, steer_table, beam_index)
    came = lax.ppermute(other, "c", [(0, 1), (1, 0)])
    own = own()
    bands = toeplitz_bands(pulse_code)
    came, bands = lax.optimization_barrier((came, bands))
    parts = lax.all_to_all(added(own, came, x_count), "x", 0, 0)
    blocks = compress(parts, bands).reshape(z_count * slabs, 2 * PAIR, LANES)
    blocks = lax.all_to_all(blocks, ("z", "y", "w"), 0, 0)
    blocks = blocks.reshape(z_count, slabs, 2 * PAIR, LANES)
    planes = clutter_filter(blocks, clutter_taps, dilation)
    return planes.reshape(2, 2, planes.shape[1], planes.shape[2])


def solution(mesh):
    split = Mesh(mesh.devices.reshape(4, 4, 2, 8, 2), ("x", "z", "c", "y", "w"))
    elem, gates = ("x", "z", "c"), ("y", "w")
    return jax.shard_map(
        on_device,
        mesh=split,
        in_specs=(P(None, elem, gates, None), P(None, None, elem), P(), P(), P(), P()),
        out_specs=P(elem, None, None, gates),
        check_vma=False,
    )
```
